32 devices in a mesh: acq: 4 (over y, x), strip: 8 (over z, core).
Axes of the slice: x: 2, y: 2, z: 4, core: 2. Of those that a mesh axis runs over, the one named last changes fastest.
Arguments:
- raw_echo_values: float32 [8, 8, 16, 120, 2, 512], P('strip', None, None, 'acq')
- cell_target_line: int32 [8, 8, 16], P('strip'), may hold values from -1 to 63, as said below
- cell_track_displacement: int32 [8, 8, 16], P('strip'), may hold values from -48 to 48
- along_track_chirp_slope: float32 [120], P('acq'), may hold values from 0.001 to 0.01
- along_track_look_radius: int32 [64], P('strip'), may hold values from 5 to 7
- range_look_radius: int32 [64], replicated, may hold values from 3 to 7
Outputs:
- coherence: float32 [120, 120, 2, 4096], P('acq', None, None, 'strip')
The draws below stay inside these ranges and needn't reach their ends.
Inputs may be any that keep to these rules, and one draw needn't show every extreme that they name: `cell_target_line`: in each reader's group of 16 slots for one strip the live slots come first; every row of every strip is named by at least one slot; some groups are full.
All inputs are finite; a program needn't handle non-finite values.
Results may differ from the reference program's by a relative error of at most 0.00065.
Values may be sent and summed in bfloat16 or wider, within the bound.
No kernel may reach another device: no remote copies, remote signals or barrier semaphores. Data moves between devices by JAX's collectives and lax.ppermute only.
A program may use at most 320 MiB of HBM per device.

```python
import jax
import jax.numpy as jnp
from jax import lax

ACQ = 120
CS = 64
COLS = 512
OMAX = 48
CAP = 16
NROWS = 512
OROWS = 64
OCOLS = 64
OPIX = 4096
N_STRIP = 8


def layout(key):
    base = jax.random.fold_in(key, 101)
    keys = jax.random.split(base, 6)
    readers = jnp.arange(N_STRIP, dtype=jnp.int32)
    counts = jax.random.randint(keys[0], (N_STRIP, N_STRIP), CAP // 2, CAP + 1)
    full_reader = jax.random.randint(keys[1], (N_STRIP,), 0, N_STRIP)
    counts = jnp.where(readers[:, None] == full_reader[None, :], CAP, counts)
    full_dest = jax.random.randint(keys[2], (), 0, N_STRIP)
    counts = jnp.where(readers[None, :] == full_dest, CAP, counts)
    small_dest = (full_dest + 1) % N_STRIP
    small_reader = (full_reader[small_dest] + 1) % N_STRIP
    counts = jnp.where((readers[:, None] == small_reader) & (readers[None, :] == small_dest), CAP // 2, counts)
    slots_all = N_STRIP * CAP
    live = jnp.arange(CAP, dtype=jnp.int32)[None, None, :] < counts[:, :, None]
    live_dest = jnp.transpose(live, (1, 0, 2)).reshape(N_STRIP, slots_all)
    orders = jax.vmap(lambda sub: jax.random.permutation(sub, slots_all))(jax.random.split(keys[3], N_STRIP))
    scores = jnp.where(live_dest, orders, orders + slots_all).astype(jnp.int32)
    ranking = jnp.argsort(jnp.argsort(scores, axis=1, stable=True), axis=1, stable=True).astype(jnp.int32)
    extra = jax.random.randint(keys[4], (N_STRIP, slots_all), 0, CS)
    dest = jnp.where(live_dest, jnp.where(ranking < CS, ranking, extra), -1)
    rows = jnp.transpose(dest.reshape(N_STRIP, N_STRIP, CAP), (1, 0, 2)).astype(jnp.int32)
    offsets = jax.random.randint(keys[5], (N_STRIP, N_STRIP, CAP), -OMAX, OMAX + 1)
    offsets = offsets.at[0, 0, 0].set(OMAX).at[0, 0, 1].set(-OMAX)
    return (rows, offsets.astype(jnp.int32))


def ramp(key):
    sub = jax.random.fold_in(key, 202)
    return jnp.exp(jax.random.uniform(sub, (ACQ,), jnp.float32, jnp.log(0.001), jnp.log(0.01)))


def draw_cell_target_line(key, part):
    rows, offsets = layout(key)
    return rows


def draw_cell_track_displacement(key, part):
    rows, offsets = layout(key)
    return offsets


def draw_along_track_chirp_slope(key, part):
    return ramp(key)


def draw_raw_echo_values(key, part):
    rows, offsets = layout(key)
    rates = ramp(key)
    key = jax.random.fold_in(key, 3)
    keys = jax.random.split(key, 3)
    scene = jax.random.normal(keys[0], (N_STRIP, CS, 2, COLS), jnp.float32)
    strips = jnp.arange(N_STRIP, dtype=jnp.int32)[None, :, None]
    common = scene[strips, jnp.clip(rows, 0, CS - 1)]
    gains = jax.random.uniform(keys[1], (ACQ,), jnp.float32, 0.5, 3.0)
    noise = jax.random.normal(keys[2], (N_STRIP, N_STRIP, CAP, ACQ, 2, COLS), jnp.float32)
    value = gains[None, None, None, :, None, None] * common[:, :, :, None] + noise
    phase = (offsets.astype(jnp.float32) ** 2)[..., None] * rates
    cosine = jnp.cos(phase)[..., None]
    sine_part = jnp.sin(phase)[..., None]
    inphase_source = value[..., 0, :]
    quadrature_source = value[..., 1, :]
    real_out = inphase_source * cosine - quadrature_source * sine_part
    imag_out = quadrature_source * cosine + inphase_source * sine_part
    return jnp.stack([real_out, imag_out], axis=-2)


def plant(result, stream_key, least, largest):
    longest = result.shape.index(max(result.shape))
    spots = []
    for shift in (0, 1):
        where = [jax.random.randint(jax.random.fold_in(stream_key, axis), (), 0, length) for axis, length in enumerate(result.shape)]
        where[longest] = (where[longest] + shift) % result.shape[longest]
        spots.append(tuple(where))
    return result.at[spots[0]].set(least).at[spots[1]].set(largest)


def setup_inputs(seed: int = 0) -> dict:
    seeds = jax.random.split(jax.random.key(seed), 7)
    return {
        "raw_echo_values": draw_raw_echo_values(jax.random.fold_in(seeds[6], 71), 0),
        "cell_target_line": draw_cell_target_line(jax.random.fold_in(seeds[6], 71), 0),
        "cell_track_displacement": draw_cell_track_displacement(jax.random.fold_in(seeds[6], 71), 0),
        "along_track_chirp_slope": draw_along_track_chirp_slope(jax.random.fold_in(seeds[6], 71), 0),
        "along_track_look_radius": plant(jax.random.randint(seeds[4], (OROWS,), 5, 8), jax.random.fold_in(seeds[4], 1), 5, 7).astype(jnp.int32),
        "range_look_radius": plant(jax.random.randint(seeds[5], (OCOLS,), 3, 8), jax.random.fold_in(seeds[5], 1), 3, 7).astype(jnp.int32),
    }


epsilon = 1e-06

def subtract_linear_chirp(raw_echo_values, cell_track_displacement, along_track_chirp_slope):
    squared = cell_track_displacement.astype(jnp.float32) ** 2
    phase = squared[..., None] * along_track_chirp_slope
    cosine = jnp.cos(phase)[..., None]
    sine_part = jnp.sin(phase)[..., None]
    inphase_source = raw_echo_values[..., 0, :]
    quadrature_source = raw_echo_values[..., 1, :]
    real_out = inphase_source * cosine + quadrature_source * sine_part
    imag_out = quadrature_source * cosine - inphase_source * sine_part
    return jnp.stack([real_out, imag_out], axis=-2)

def windows_of(padded):
    inner = padded.shape[2] - 8
    acq_count = padded.shape[0]
    columns = padded.shape[3]
    upper = padded[:, :, :inner].reshape(acq_count, 2, inner // 8, 8, columns)
    lower = padded[:, :, 8:].reshape(acq_count, 2, inner // 8, 8, columns)
    return jnp.concatenate([upper, lower], axis=3)

def look(values, colmask):
    return jnp.einsum('...c,cq->...q', values, colmask, precision=lax.Precision.HIGHEST)

def power_of(win, weight):
    return jnp.einsum('apojc,apojc->aoc', win * weight[None, None, :, :, None], win, preferred_element_type=jnp.float32, precision=lax.Precision.HIGHEST)

def coherence_block(left_win, left_power, right_win, weight, colmask):
    weighted = left_win * weight[None, None, :, :, None]
    swapped = jnp.stack([weighted[:, 1], -weighted[:, 0]], axis=1)
    real_sum = jnp.einsum('apojc,bpojc->aboc', weighted, right_win, preferred_element_type=jnp.float32, precision=lax.Precision.HIGHEST)
    imag_sum = jnp.einsum('apojc,bpojc->aboc', swapped, right_win, preferred_element_type=jnp.float32, precision=lax.Precision.HIGHEST)
    right_power = look(power_of(right_win, weight), colmask)
    scale = 1.0 / jnp.sqrt(left_power[:, None] * right_power[None] + epsilon)
    real_look = look(real_sum, colmask) * scale
    imag_look = look(imag_sum, colmask) * scale
    stacked = jnp.stack([real_look, imag_look], axis=2)
    return stacked.reshape(stacked.shape[0], stacked.shape[1], 2, -1)

def make_masks(along_track_look_radius, range_look_radius, columns, out_cols):
    offsets_row = jnp.abs(jnp.arange(16, dtype=jnp.int32) - 8)
    weight = (offsets_row[None, :] <= along_track_look_radius[:, None]).astype(jnp.float32)
    centres = 8 * jnp.arange(out_cols, dtype=jnp.int32) + 4
    distance = jnp.abs(jnp.arange(columns, dtype=jnp.int32)[:, None] - centres[None, :])
    colmask = (distance <= range_look_radius[None, :]).astype(jnp.float32)
    return (weight, colmask)

def reference(raw_echo_values, cell_target_line, cell_track_displacement, along_track_chirp_slope, along_track_look_radius, range_look_radius):
    levelled_echoes = subtract_linear_chirp(raw_echo_values, cell_track_displacement, along_track_chirp_slope).astype(jnp.bfloat16).astype(jnp.float32)
    onehot = (jnp.transpose(cell_target_line, (1, 0, 2))[:, None, :, :] == jnp.arange(CS, dtype=jnp.int32)[None, :, None, None]).astype(jnp.float32)
    counts = lax.optimization_barrier(jnp.sum(onehot, axis=(2, 3)))
    summed = jnp.einsum('sxrk,rskapc->apsxc', onehot, levelled_echoes, precision=lax.Precision.HIGHEST)
    tile = (summed / counts[None, None, :, :, None]).reshape(ACQ, 2, NROWS, COLS).astype(jnp.bfloat16)
    padded = jnp.pad(tile, ((0, 0), (0, 0), (4, 4), (0, 0)))
    weight_all, colmask = make_masks(along_track_look_radius, range_look_radius, COLS, OCOLS)
    per_strip = CS // 8

    def one_strip(index):
        rows = lax.dynamic_slice_in_dim(padded, (index * CS).astype(jnp.int32), CS + 8, 2)
        win = windows_of(rows).astype(jnp.float32)
        weight = lax.dynamic_slice_in_dim(weight_all, (index * per_strip).astype(jnp.int32), per_strip, 0)
        power = look(power_of(win, weight), colmask)
        return coherence_block(win, power, win, weight, colmask)
    blocks = lax.map(one_strip, jnp.arange(N_STRIP, dtype=jnp.int32))
    blocks = blocks.reshape(N_STRIP, ACQ, ACQ, 2, per_strip * OCOLS)
    return jnp.transpose(blocks, (1, 2, 3, 0, 4)).reshape(ACQ, ACQ, 2, OPIX)
```

```python
import functools

import jax
import jax.numpy as jnp
from jax import lax
from jax.experimental import pallas as pl
from jax.experimental.pallas import tpu as pltpu
from jax.sharding import PartitionSpec as P

epsilon = 1e-06
LANES = 128
F32 = jnp.float32
BF16 = jnp.bfloat16


def work(microseconds):
    return pl.CostEstimate(
        flops=int(microseconds * 1e9), bytes_accessed=int(microseconds * 1e6), transcendentals=0
    )


def params(**more):
    return pltpu.CompilerParams(vmem_limit_bytes=56 * 1024 * 1024, **more)


def sublane_exchange(arrays, row, wanted):
    known = {}

    def value(level, i):
        if level == 0:
            return arrays[i]
        if (level, i) not in known:
            step = 8 >> level
            keep = (row // step) % 2 == (1 if i & step else 0)
            shift = 8 - step if i & step else step
            other = pltpu.roll(value(level - 1, i ^ step), shift, 0)
            known[level, i] = jnp.where(keep, value(level - 1, i), other)
        return known[level, i]

    return [value(3, i) for i in wanted]


def deramp_kernel(acqs, chosen, with_lines, *refs):
    raw_ref, cos_ref, sin_ref = refs[:3]
    lines_ref = refs[3] if with_lines else None
    outs = refs[4:] if with_lines else refs[3:]
    cap = cos_ref.shape[1]
    row = lax.broadcasted_iota(jnp.int32, (8, LANES), 0)
    wanted = [2 * g + part for g in chosen for part in range(2)]
    cosines = cos_ref[0]
    sines = sin_ref[0]
    for a in range(acqs):
        halves = []
        for first in range(0, cap, 8):
            cosine = jnp.broadcast_to(cosines[first : first + 8, a : a + 1], (8, LANES))
            sine = jnp.broadcast_to(sines[first : first + 8, a : a + 1], (8, LANES))
            if len(wanted) == 2:
                values = [
                    raw_ref[pl.ds((first * acqs + a) * 8 + w, 8, stride=acqs * 8), :]
                    for w in wanted
                ]
            else:
                starts = [((first + i) * acqs + a) * 8 for i in range(8)]
                loaded = [raw_ref[start : start + 8, :] for start in starts]
                values = sublane_exchange(loaded, row, wanted)
            done = []
            for real, imag in zip(values[::2], values[1::2]):
                done += [real * cosine + imag * sine, imag * cosine - real * sine]
            halves.append(done)
        for index, out in enumerate(outs):
            for part in range(2):
                pieces = [half[2 * index + part] for half in halves]
                out[0, part * acqs + a] = jnp.concatenate(pieces, axis=0).astype(BF16)
    if with_lines:
        lines = lines_ref[pl.ds(pl.program_id(0), 1), :].astype(F32)
        slot = lax.broadcasted_iota(jnp.int32, (cap, cap), 0)
        same = slot == lax.broadcasted_iota(jnp.int32, (cap, cap), 1)
        lines = jnp.sum(jnp.where(same, lines, 0.0), axis=1, keepdims=True)
        lines = jnp.broadcast_to(lines, (cap, LANES))
        outs[0][0, 2 * acqs] = lines.astype(BF16)


def deramp(raw, cosine, sine, chosen, lines=None):
    _, strips, cap, acqs, _, columns = raw.shape
    groups = columns // LANES
    view = raw.reshape(strips * cap, acqs, 2, groups, LANES)
    view = view.transpose(0, 1, 3, 2, 4).reshape(strips * cap * acqs * groups * 2, LANES)
    block = cap * acqs * groups * 2
    pieces = 2 * acqs + (lines is not None)
    out = jax.ShapeDtypeStruct((strips, pieces, cap, LANES), BF16)
    args = [view, cosine, sine]
    in_specs = [
        pl.BlockSpec((block, LANES), lambda i: (i, 0)),
        pl.BlockSpec((1, cap, acqs), lambda i: (i, 0, 0)),
        pl.BlockSpec((1, cap, acqs), lambda i: (i, 0, 0)),
    ]
    if lines is not None:
        args.append(lines)
        in_specs.append(pl.BlockSpec((strips, cap), lambda i: (0, 0)))
    return pl.pallas_call(
        functools.partial(deramp_kernel, acqs, chosen, lines is not None),
        grid=(strips,),
        in_specs=in_specs,
        out_specs=[pl.BlockSpec((1, pieces, cap, LANES), lambda i: (i, 0, 0, 0))] * len(chosen),
        out_shape=[out] * len(chosen),
        compiler_params=params(),
        name=f"deramp{chosen[0]}",
        cost_estimate=work(6 if lines is not None else 9),
    )(*args)


def tile_kernel(acqs, padded, lines_ref, data_ref, out_ref, top_ref, bottom_ref, scratch):
    readers, _, cap, _ = data_ref.shape
    slots = readers * cap
    strip_rows = out_ref.shape[0]

    def piece(ref, index):
        value = ref[:, index]
        if cap % 16:
            return value.astype(F32).reshape(slots, LANES).astype(BF16)
        return value.reshape(slots, LANES)

    target = lax.broadcasted_iota(jnp.int32, (slots, LANES), 1).astype(F32)
    selector = jnp.where(piece(lines_ref, 0).astype(F32) == target, 1.0, 0.0)
    selector = selector.astype(F32).T[:strip_rows]
    counts = jnp.broadcast_to(
        jnp.sum(selector, axis=1, keepdims=True), (strip_rows, LANES)
    )
    onehot = selector.astype(BF16)
    zeros = jnp.zeros((strip_rows, LANES), F32)
    for part in range(2):
        for a in range(acqs):
            summed = jnp.dot(
                onehot, piece(data_ref, part * acqs + a), preferred_element_type=F32
            )
            scratch[pl.ds(part * padded + a, strip_rows, stride=2 * padded), :] = pltpu.roll(
                summed / counts, 4, 1
            )
        for a in range(acqs, padded):
            scratch[pl.ds(part * padded + a, strip_rows, stride=2 * padded), :] = zeros
    for x in range(strip_rows):
        value = scratch[pl.ds(x * 2 * padded, 2 * padded), :].astype(BF16)
        out_ref[x] = value
        if x < 4:
            top_ref[x] = value
        if x >= strip_rows - 4:
            bottom_ref[x - strip_rows + 4] = value


def make_tile(lines, data, acqs, padded, strip_rows):
    readers, pieces, cap, _ = data.shape
    whole = (readers, pieces, cap, LANES)
    return pl.pallas_call(
        functools.partial(tile_kernel, acqs, padded),
        grid=(1,),
        in_specs=[
            pl.BlockSpec((readers, 1, cap, LANES), lambda i: (0, 2 * acqs, 0, 0)),
            pl.BlockSpec(whole, lambda i: (0, 0, 0, 0)),
        ],
        out_specs=[
            pl.BlockSpec((n, 2 * padded, LANES), lambda i: (0, 0, 0)) for n in (strip_rows, 4, 4)
        ],
        out_shape=[
            jax.ShapeDtypeStruct((n, 2 * padded, LANES), BF16) for n in (strip_rows, 4, 4)
        ],
        scratch_shapes=[pltpu.VMEM((strip_rows * 2 * padded, LANES), F32)],
        compiler_params=params(),
        name="tile",
        cost_estimate=work(4),
    )(lines, data)


def block_exchange(arrays, lane):
    arrays = list(arrays)
    for step in (4, 2, 1):
        mask = (lane // (16 * step)) % 2 == 0
        new = list(arrays)
        for i in range(8):
            if i & step:
                continue
            low, high = arrays[i], arrays[i + step]
            new[i] = jnp.where(mask, low, pltpu.roll(high, 16 * step, 1))
            new[i + step] = jnp.where(
                mask, pltpu.roll(low, LANES - 16 * step, 1), high
            )
        arrays = new
    return arrays


def pairs_kernel(k, last, sources, padded, *refs):
    refs = list(refs)
    radius_ref, mask_ref, cmask_ref = refs[:3]
    del refs[:3]
    halos = refs[: len(sources[0])]
    del refs[: len(sources[0])]
    count = 1 + max(index for part in sources for index, _ in part)
    blocks = refs[: 2 * count]
    del refs[: 2 * count]
    first = k == 0
    edge_ref = None
    if not first:
        before = refs[:2]
        before_halo_ref, edge_ref = refs[2:4]
        del refs[:5]
    sums_ref = refs.pop(0)
    edge_out = None if last else refs.pop(0)
    even, odd, over, left, left_over, power, staged, sems = refs

    y = pl.program_id(0)
    out_rows = radius_ref.shape[0]
    rows2 = 2 * padded
    width = 2 * LANES
    slots = 17 if last else 16
    low = 1 if first else 0
    q0 = 16 * k - 1 + low
    lane = lax.broadcasted_iota(jnp.int32, (rows2, LANES), 1)
    early = lax.broadcasted_iota(jnp.int32, (8, width), 0) < 4

    def weight(o, j):
        o = jnp.clip(o, 0, out_rows - 1)
        return jnp.where(radius_ref[o] >= abs(j - 8), 1.0, 0.0).astype(F32)

    def squares(value):
        return value[:, :LANES] * value[:, :LANES] + value[:, LANES:] * value[:, LANES:]

    at_top = y == 0
    at_bottom = y == out_rows

    def rows_of(low_ref, high_ref, halo, xx, size):
        main = low_ref[xx, size, :] if xx < 4 else high_ref[xx - 4, size, :]
        edge = at_top if xx < 4 else at_bottom
        return jnp.where(edge, halo.astype(F32), main.astype(F32))

    slot_now = lax.rem(y, 2)
    slot_old = 1 - slot_now
    for xx in range(8):
        x = y * 8 + xx
        parts = []
        for number, part in enumerate(sources):
            pieces = [
                rows_of(
                    blocks[2 * index],
                    blocks[2 * index + 1],
                    halos[i][xx, number * padded : (number + 1) * padded, :],
                    xx,
                    slice(offset, offset + padded),
                )
                for i, (index, offset) in enumerate(part)
            ]
            parts.append(jnp.concatenate(pieces, axis=0).T)
        value = jnp.concatenate(parts, axis=1)
        top = value[:8]
        bottom = value[LANES - 8 :]
        if first:
            tail = jnp.zeros((8, width), F32)
            proper = value
        else:
            tail = edge_ref[xx, :8]
            start = jnp.where(early, edge_ref[xx, 8:], top)
            proper = jnp.concatenate([start, value[8:]], axis=0)
        even[x] = proper.reshape(8, 16, width).astype(BF16)
        shifted = jnp.concatenate([tail, proper[: LANES - 8]], axis=0)
        odd[x] = shifted.reshape(8, 16, width).astype(BF16)
        levels = [squares(tail), squares(proper)]
        if last:
            over[x] = jnp.concatenate([bottom, top], axis=0).astype(BF16)
            levels.append(squares(top))
        else:
            edge_out[xx, :8] = bottom
            edge_out[xx, 8:] = top
        level = jnp.concatenate(levels, axis=0)
        new = weight(y, xx) * level
        old = weight(y - 1, xx + 8) * level
        if xx == 0:
            power[slot_now] = new
        else:
            power[slot_now] = power[slot_now] + new
        power[slot_old] = power[slot_old] + old

    raw = [
        rows_of(blocks[0], blocks[1], halos[0][xx], xx, slice(None)) for xx in range(8)
    ]
    owned = raw
    rolled = [pltpu.roll(value, 8, 1) for value in owned]
    if not first:
        before = [
            rows_of(before[0], before[1], before_halo_ref[xx], xx, slice(None))
            for xx in range(8)
        ]
        owned = [jnp.where(lane < 4, before[xx], raw[xx]) for xx in range(8)]
        rolled = [pltpu.roll(value, 8, 1) for value in owned]
        rolled = [
            jnp.where(lane < 8, pltpu.roll(before[xx], 8, 1), rolled[xx]) for xx in range(8)
        ]
    for tile, value in enumerate(block_exchange(owned, lane)):
        left[slot_now, 0, tile] = value
    for tile, value in enumerate(block_exchange(rolled, lane)):
        left[slot_now, 1, tile] = value
    if last:
        total = None
        for xx in range(8):
            value = pltpu.roll(raw[xx], 8 + 16 * xx, 1)
            total = value if total is None else jnp.where(lane // 16 == xx, value, total)
        left_over[slot_now] = total

    @pl.when(y > 0)
    def _():
        o = y - 1
        buffer = lax.rem(o, 2)

        def send(row, which):
            return pltpu.make_async_copy(
                staged.at[which, pl.ds(low, slots - low)],
                sums_ref.at[row, pl.ds(q0, slots - low)],
                sems.at[which],
            )

        @pl.when(o >= 2)
        def _():
            send(o - 2, buffer).wait()

        for i in range(low, slots):
            if i == 16:
                right = over[pl.ds(o * 8, 16)].reshape(256, width)
                sides = [left_over[slot_old], left_over[slot_now]]
            else:
                tile, shift = (i // 2, 1) if i % 2 == 0 else ((i - 1) // 2, 0)
                source = odd if shift else even
                right = source[pl.ds(o * 8, 16), tile].reshape(256, width)
                sides = [left[slot_old, shift, tile], left[slot_now, shift, tile]]
            row = 16 * k + i
            mask = mask_ref[0, row : row + 1, :]
            weighted = (jnp.concatenate(sides, axis=1) * mask).astype(BF16)
            product = jnp.dot(weighted, right, preferred_element_type=F32)
            real = product[:padded, :LANES] + product[padded:, LANES:]
            imag = product[padded:, :LANES] - product[:padded, LANES:]
            energy = jnp.sum(
                cmask_ref[row] * power[slot_old, pl.ds(8 * i, 16), :], axis=0, keepdims=True
            )
            staged[buffer, i, :padded] = real
            staged[buffer, i, padded:] = imag
            staged[buffer, i, padded - 1 : padded] = energy
        send(o, buffer).start()

        @pl.when(o == out_rows - 1)
        def _():
            if out_rows > 1:
                send(o - 1, 1 - buffer).wait()
            send(o, buffer).wait()


def pair_sums(
    k, last, radius, mask, cmask, halos, blocks, sources, before, before_halo, edge, sums
):
    strip_rows, rows2, _ = blocks[0].shape
    rows = strip_rows + 8
    padded = rows2 // 2
    width = 2 * LANES
    out_rows = radius.shape[0]
    first = k == 0
    top = strip_rows // 4 - 1

    def by_rows(array):
        return pl.BlockSpec((8, *array.shape[1:]), lambda y: (y, 0, 0))

    def by_halves(array):
        block = (4, *array.shape[1:])
        return [
            pl.BlockSpec(block, lambda y: (jnp.maximum(2 * y - 1, 0), 0, 0)),
            pl.BlockSpec(block, lambda y: (jnp.minimum(2 * y, top), 0, 0)),
        ]

    def whole(array):
        return pl.BlockSpec(array.shape, lambda y: (0,) * array.ndim)

    edge_shape = jax.ShapeDtypeStruct((rows, 16, width), F32)
    args = [radius, mask, cmask, *halos]
    in_specs = [
        pl.BlockSpec(memory_space=pltpu.SMEM),
        pl.BlockSpec((1, *mask.shape[1:]), lambda y: (jnp.maximum(y - 1, 0), 0, 0)),
        whole(cmask),
        *[whole(halo) for halo in halos],
    ]
    for block in blocks:
        args += [block, block]
        in_specs += by_halves(block)
    if not first:
        args += [before, before, before_halo, edge]
        in_specs += [*by_halves(before), whole(before_halo), by_rows(edge)]
    aliases = {}
    if not first:
        args.append(sums)
        in_specs.append(pl.BlockSpec(memory_space=pl.ANY))
        aliases[len(args) - 1] = 0
    out_cols = cmask.shape[0] - 1
    out_shape = [jax.ShapeDtypeStruct((out_rows, out_cols, rows2, LANES), F32)]
    out_specs = [pl.BlockSpec(memory_space=pl.ANY)]
    if not last:
        out_shape.append(edge_shape)
        out_specs.append(by_rows(edge_shape))
    outs = pl.pallas_call(
        functools.partial(pairs_kernel, k, last, sources, padded),
        grid=(rows // 8,),
        in_specs=in_specs,
        out_specs=out_specs,
        out_shape=out_shape,
        input_output_aliases=aliases,
        scratch_shapes=[
            pltpu.VMEM((rows, 8, 16, width), BF16),
            pltpu.VMEM((rows, 8, 16, width), BF16),
            pltpu.VMEM((rows if last else 8, 16, width), BF16),
            pltpu.VMEM((2, 2, 8, rows2, LANES), F32),
            pltpu.VMEM((2, rows2, LANES), F32),
            pltpu.VMEM((2, 144 if last else 136, LANES), F32),
            pltpu.VMEM((2, 17, rows2, LANES), F32),
            pltpu.SemaphoreType.DMA((2,)),
        ],
        compiler_params=params(),
        name=f"pairs{k}",
        cost_estimate=work(16),
    )(*args)
    return (outs[0], None) if last else (outs[0], outs[1])


def finish_kernel(acqs, padded, groups, me_ref, real_ref, imag_ref, energy_ref, out_ref, power):
    step = pl.program_id(0)
    me = me_ref[0]
    out_rows, out_cols, _, _ = real_ref.shape
    pixels = out_rows * out_cols
    lane_groups = pixels // LANES

    def strided(ref, g, row):
        return ref.reshape(pixels * 8, LANES)[pl.ds(g * LANES * 8 + row, LANES, stride=8), :]

    @pl.when(step == 0)
    def _():
        for g in range(lane_groups):
            power[g] = strided(energy_ref, g, 7).T

    for m in range(8):
        for g in range(lane_groups):
            mine = power[g, pl.ds(step * 8 + m, 1), :]
            scale = lax.rsqrt(power[g] * mine + epsilon)
            for part, ref in enumerate((real_ref, imag_ref)):
                value = strided(ref, g, m).T * scale
                for i in range(groups):
                    start = lax.bitwise_xor(me, i) * (acqs * 2 * lane_groups)
                    out_ref[
                        m, pl.ds(start + 2 * g + part, acqs, stride=2 * lane_groups), :
                    ] = value[i * padded : i * padded + acqs]


def finish(me, sums, acqs, groups):
    out_rows, out_cols, rows2, _ = sums.shape
    padded = rows2 // 2
    lane_groups = out_rows * out_cols // LANES
    total = acqs * groups
    blocks = padded // 8

    def spec(index):
        return pl.BlockSpec((out_rows, out_cols, 8, LANES), index)

    out = pl.pallas_call(
        functools.partial(finish_kernel, acqs, padded, groups),
        grid=(pl.cdiv(acqs, 8),),
        in_specs=[
            pl.BlockSpec(memory_space=pltpu.SMEM),
            spec(lambda i: (0, 0, i, 0)),
            spec(lambda i: (0, 0, i + blocks, 0)),
            spec(lambda i: (0, 0, blocks - 1, 0)),
        ],
        out_specs=pl.BlockSpec((8, total * 2 * lane_groups, LANES), lambda i: (i, 0, 0)),
        out_shape=jax.ShapeDtypeStruct((acqs, total * 2 * lane_groups, LANES), F32),
        scratch_shapes=[pltpu.VMEM((lane_groups, LANES, LANES), F32)],
        compiler_params=params(),
        name="finish",
        cost_estimate=pl.CostEstimate(
            flops=6 * sums.size, bytes_accessed=8 * sums.size, transcendentals=sums.size // 2
        ),
    )(me, sums, sums, sums)
    out = out.reshape(acqs, total, lane_groups, 2, LANES).transpose(0, 1, 3, 2, 4)
    return out.reshape(acqs, total, 2, lane_groups * LANES)


def exchange(value, axis, bit):
    size = lax.axis_size(axis)
    return lax.ppermute(value, axis, [(i, i ^ bit) for i in range(size)])


def neighbours(top, bottom):
    devices = lax.axis_size("strip")
    up = [(i, i + 1) for i in range(devices - 1)]
    down = [(j, i) for i, j in up]
    before = lax.ppermute(bottom, "strip", up)
    after = lax.ppermute(top, "strip", down)
    return jnp.concatenate([before, after], axis=0)


def after(value, *others):
    return lax.optimization_barrier((value, *others))[0]


def gathered(own, padded, filler=()):
    groups = lax.axis_size("acq")
    if groups != 4:
        blocks = [own] + [exchange(own, "acq", bit) for bit in range(1, groups)]
        return blocks, [[(i, part * padded) for i in range(groups)] for part in range(2)]
    one = exchange(own, "acq", 1)
    two = exchange(own, "acq", 2)
    real = exchange(after(two[:, :padded], *filler), "acq", 1)
    imag = exchange(after(one[:, padded:], *filler), "acq", 2)
    blocks = [own, one, two, real, imag]
    shared = [[(i, part * padded) for i in range(3)] for part in range(2)]
    return blocks, [shared[0] + [(3, 0)], shared[1] + [(4, 0)]]


def per_device(
    raw_echo_values,
    cell_target_line,
    cell_track_displacement,
    along_track_chirp_slope,
    along_track_look_radius,
    range_look_radius,
):
    _, strips, cap, acqs, _, columns = raw_echo_values.shape
    groups = lax.axis_size("acq")
    padded = LANES // groups
    out_rows = along_track_look_radius.shape[0]
    out_cols = range_look_radius.shape[0]
    strip_rows = out_rows * 8
    chunks = columns // LANES
    me = lax.axis_index("acq").astype(jnp.int32).reshape(1)

    squared = cell_track_displacement[0].astype(F32) ** 2
    phase = squared[..., None] * along_track_chirp_slope
    cosine, sine = jnp.cos(phase), jnp.sin(phase)
    sent = deramp(raw_echo_values, cosine, sine, [0], cell_target_line[0])
    sent += deramp(raw_echo_values, cosine, sine, list(range(1, chunks)))

    inner = jnp.arange(16, dtype=jnp.int32)
    row_mask = jnp.abs(inner - 8)[None, :] <= along_track_look_radius[:, None]
    column = 8 * jnp.arange(out_cols, dtype=jnp.int32)[:, None] - 4 + inner[None, :]
    col_mask = jnp.abs(inner - 8)[None, :] <= range_look_radius[:, None]
    col_mask = col_mask & (column >= 0) & (column < columns)
    col_mask = jnp.pad(col_mask, ((1, 0), (0, 0)))
    mask = (row_mask[:, None, :, None] & col_mask[None, :, None, :]).astype(F32)
    mask = mask.reshape(out_rows, out_cols + 1, 256)
    cmask = jnp.broadcast_to(col_mask.astype(F32)[:, :, None], (out_cols + 1, 16, LANES))

    received = []

    def receive(k, *others):
        piece = after(sent[k], *others) if others else sent[k]
        received.append(
            lax.all_to_all(piece, "strip", split_axis=0, concat_axis=0, tiled=True)
        )

    def spread(halo):
        return [halo] + [exchange(halo, "acq", bit) for bit in range(1, groups)]

    receive(0)
    receive(1, received[0])
    edge = sums = None
    waiting = None
    previous = (None, None)
    for k in range(chunks):
        final = k == chunks - 1
        own, top, bottom = make_tile(received[0], received[k], acqs, padded, strip_rows)
        if waiting is not None:
            halos = spread(previous[1])
            own = after(own, *halos)
            sums, edge = pair_sums(*waiting[:5], halos, *waiting[5:], edge, sums)
        if final:
            halo = neighbours(top, bottom)
            blocks, sources = gathered(own, padded)
        else:
            blocks, sources = gathered(own, padded)
            halo = neighbours(after(top, *blocks), after(bottom, *blocks))
        if k + 2 < chunks:
            receive(k + 2, received[k + 1], halo)
        waiting = (
            k,
            final,
            along_track_look_radius,
            mask,
            cmask,
            blocks,
            sources,
            *previous,
        )
        previous = (own, halo)
    sums, edge = pair_sums(*waiting[:5], spread(previous[1]), *waiting[5:], edge, sums)
    return finish(me, sums, acqs, groups)


def solution(mesh):
    placed = (
        P("strip", None, None, "acq", None, None),
        P("strip", None, None),
        P("strip", None, None),
        P("acq"),
        P("strip"),
        P(),
    )
    return jax.shard_map(
        per_device,
        mesh=mesh,
        in_specs=placed,
        out_specs=P("acq", None, None, "strip"),
        check_vma=False,
    )
```

```python
import functools

import jax
import jax.numpy as jnp
from jax import lax
from jax.experimental import pallas as pl
from jax.experimental.pallas import tpu as pltpu
from jax.sharding import PartitionSpec as P

epsilon = 1e-06
LANES = 128
F32 = jnp.float32
BF16 = jnp.bfloat16


def work(microseconds):
    return pl.CostEstimate(
        flops=int(microseconds * 1e9), bytes_accessed=int(microseconds * 1e6), transcendentals=0
    )


def params(**more):
    return pltpu.CompilerParams(vmem_limit_bytes=56 * 1024 * 1024, **more)


def sublane_exchange(arrays, row, wanted):
    known = {}

    def value(level, i):
        if level == 0:
            return arrays[i]
        if (level, i) not in known:
            step = 8 >> level
            keep = (row // step) % 2 == (1 if i & step else 0)
            shift = 8 - step if i & step else step
            other = pltpu.roll(value(level - 1, i ^ step), shift, 0)
            known[level, i] = jnp.where(keep, value(level - 1, i), other)
        return known[level, i]

    return [value(3, i) for i in wanted]


def deramp_kernel(acqs, chosen, with_lines, *refs):
    raw_ref, cos_ref, sin_ref = refs[:3]
    lines_ref = refs[3] if with_lines else None
    outs = refs[4:] if with_lines else refs[3:]
    cap = cos_ref.shape[1]
    row = lax.broadcasted_iota(jnp.int32, (8, LANES), 0)
    wanted = [2 * g + part for g in chosen for part in range(2)]
    cosines = cos_ref[0]
    sines = sin_ref[0]
    for a in range(acqs):
        halves = []
        for first in range(0, cap, 8):
            cosine = jnp.broadcast_to(cosines[first : first + 8, a : a + 1], (8, LANES))
            sine = jnp.broadcast_to(sines[first : first + 8, a : a + 1], (8, LANES))
            if len(wanted) == 2:
                values = [
                    raw_ref[pl.ds((first * acqs + a) * 8 + w, 8, stride=acqs * 8), :]
                    for w in wanted
                ]
            else:
                starts = [((first + i) * acqs + a) * 8 for i in range(8)]
                loaded = [raw_ref[start : start + 8, :] for start in starts]
                values = sublane_exchange(loaded, row, wanted)
            done = []
            for real, imag in zip(values[::2], values[1::2]):
                done += [real * cosine + imag * sine, imag * cosine - real * sine]
            halves.append(done)
        for index, out in enumerate(outs):
            for part in range(2):
                pieces = [half[2 * index + part] for half in halves]
                out[0, part * acqs + a] = jnp.concatenate(pieces, axis=0).astype(BF16)
    if with_lines:
        lines = lines_ref[pl.ds(pl.program_id(0), 1), :].astype(F32)
        slot = lax.broadcasted_iota(jnp.int32, (cap, cap), 0)
        same = slot == lax.broadcasted_iota(jnp.int32, (cap, cap), 1)
        lines = jnp.sum(jnp.where(same, lines, 0.0), axis=1, keepdims=True)
        lines = jnp.broadcast_to(lines, (cap, LANES))
        outs[0][0, 2 * acqs] = lines.astype(BF16)


def deramp(raw, cosine, sine, chosen, lines=None):
    _, strips, cap, acqs, _, columns = raw.shape
    groups = columns // LANES
    view = raw.reshape(strips * cap, acqs, 2, groups, LANES)
    view = view.transpose(0, 1, 3, 2, 4).reshape(strips * cap * acqs * groups * 2, LANES)
    block = cap * acqs * groups * 2
    pieces = 2 * acqs + (lines is not None)
    out = jax.ShapeDtypeStruct((strips, pieces, cap, LANES), BF16)
    args = [view, cosine, sine]
    in_specs = [
        pl.BlockSpec((block, LANES), lambda i: (i, 0)),
        pl.BlockSpec((1, cap, acqs), lambda i: (i, 0, 0)),
        pl.BlockSpec((1, cap, acqs), lambda i: (i, 0, 0)),
    ]
    if lines is not None:
        args.append(lines)
        in_specs.append(pl.BlockSpec((strips, cap), lambda i: (0, 0)))
    return pl.pallas_call(
        functools.partial(deramp_kernel, acqs, chosen, lines is not None),
        grid=(strips,),
        in_specs=in_specs,
        out_specs=[pl.BlockSpec((1, pieces, cap, LANES), lambda i: (i, 0, 0, 0))] * len(chosen),
        out_shape=[out] * len(chosen),
        compiler_params=params(),
        name=f"deramp{chosen[0]}",
        cost_estimate=work(6 if lines is not None else 9),
    )(*args)


def tile_kernel(acqs, padded, lines_ref, data_ref, out_ref, top_ref, bottom_ref, scratch):
    readers, _, cap, _ = data_ref.shape
    slots = readers * cap
    strip_rows = out_ref.shape[0]

    def piece(ref, index):
        value = ref[:, index]
        if cap % 16:
            return value.astype(F32).reshape(slots, LANES).astype(BF16)
        return value.reshape(slots, LANES)

    target = lax.broadcasted_iota(jnp.int32, (slots, LANES), 1).astype(F32)
    selector = jnp.where(piece(lines_ref, 0).astype(F32) == target, 1.0, 0.0)
    selector = selector.astype(F32).T[:strip_rows]
    counts = jnp.broadcast_to(
        jnp.sum(selector, axis=1, keepdims=True), (strip_rows, LANES)
    )
    onehot = selector.astype(BF16)
    zeros = jnp.zeros((strip_rows, LANES), F32)
    for part in range(2):
        for a in range(acqs):
            summed = jnp.dot(
                onehot, piece(data_ref, part * acqs + a), preferred_element_type=F32
            )
            scratch[pl.ds(part * padded + a, strip_rows, stride=2 * padded), :] = pltpu.roll(
                summed / counts, 4, 1
            )
        for a in range(acqs, padded):
            scratch[pl.ds(part * padded + a, strip_rows, stride=2 * padded), :] = zeros
    for x in range(strip_rows):
        value = scratch[pl.ds(x * 2 * padded, 2 * padded), :].astype(BF16)
        out_ref[x] = value
        if x < 4:
            top_ref[x] = value
        if x >= strip_rows - 4:
            bottom_ref[x - strip_rows + 4] = value


def make_tile(lines, data, acqs, padded, strip_rows):
    readers, pieces, cap, _ = data.shape
    whole = (readers, pieces, cap, LANES)
    return pl.pallas_call(
        functools.partial(tile_kernel, acqs, padded),
        grid=(1,),
        in_specs=[
            pl.BlockSpec((readers, 1, cap, LANES), lambda i: (0, 2 * acqs, 0, 0)),
            pl.BlockSpec(whole, lambda i: (0, 0, 0, 0)),
        ],
        out_specs=[
            pl.BlockSpec((n, 2 * padded, LANES), lambda i: (0, 0, 0)) for n in (strip_rows, 4, 4)
        ],
        out_shape=[
            jax.ShapeDtypeStruct((n, 2 * padded, LANES), BF16) for n in (strip_rows, 4, 4)
        ],
        scratch_shapes=[pltpu.VMEM((strip_rows * 2 * padded, LANES), F32)],
        compiler_params=params(),
        name="tile",
        cost_estimate=work(4),
    )(lines, data)


def block_exchange(arrays, lane):
    arrays = list(arrays)
    for step in (4, 2, 1):
        mask = (lane // (16 * step)) % 2 == 0
        new = list(arrays)
        for i in range(8):
            if i & step:
                continue
            low, high = arrays[i], arrays[i + step]
            new[i] = jnp.where(mask, low, pltpu.roll(high, 16 * step, 1))
            new[i + step] = jnp.where(
                mask, pltpu.roll(low, LANES - 16 * step, 1), high
            )
        arrays = new
    return arrays


def pairs_kernel(k, last, sources, padded, *refs):
    refs = list(refs)
    radius_ref, mask_ref, cmask_ref = refs[:3]
    del refs[:3]
    halos = refs[: len(sources[0])]
    del refs[: len(sources[0])]
    count = 1 + max(index for part in sources for index, _ in part)
    blocks = refs[: 2 * count]
    del refs[: 2 * count]
    first = k == 0
    edge_ref = None
    if not first:
        before = refs[:2]
        before_halo_ref, edge_ref = refs[2:4]
        del refs[:5]
    sums_ref = refs.pop(0)
    edge_out = None if last else refs.pop(0)
    even, odd, over, left, left_over, power, staged, sems = refs

    y = pl.program_id(0)
    out_rows = radius_ref.shape[0]
    rows2 = 2 * padded
    width = 2 * LANES
    slots = 17 if last else 16
    low = 1 if first else 0
    q0 = 16 * k - 1 + low
    lane = lax.broadcasted_iota(jnp.int32, (rows2, LANES), 1)
    early = lax.broadcasted_iota(jnp.int32, (8, width), 0) < 4

    def weight(o, j):
        o = jnp.clip(o, 0, out_rows - 1)
        return jnp.where(radius_ref[o] >= abs(j - 8), 1.0, 0.0).astype(F32)

    def squares(value):
        return value[:, :LANES] * value[:, :LANES] + value[:, LANES:] * value[:, LANES:]

    at_top = y == 0
    at_bottom = y == out_rows

    def rows_of(low_ref, high_ref, halo, xx, size):
        main = low_ref[xx, size, :] if xx < 4 else high_ref[xx - 4, size, :]
        edge = at_top if xx < 4 else at_bottom
        return jnp.where(edge, halo, main)

    slot_now = lax.rem(y, 2)
    slot_old = 1 - slot_now
    for xx in range(8):
        x = y * 8 + xx
        parts = []
        for number, part in enumerate(sources):
            pieces = [
                rows_of(
                    blocks[2 * index],
                    blocks[2 * index + 1],
                    halos[i][xx, number * padded : (number + 1) * padded, :],
                    xx,
                    slice(offset, offset + padded),
                )
                for i, (index, offset) in enumerate(part)
            ]
            parts.append(jnp.concatenate(pieces, axis=0).T)
        narrow = jnp.concatenate(parts, axis=1)
        value = narrow.astype(F32)
        top = value[:8]
        bottom = value[LANES - 8 :]
        if first:
            tail = jnp.zeros((8, width), F32)
            proper = value
        else:
            tail = edge_ref[xx, :8]
            start = jnp.where(early, edge_ref[xx, 8:], top)
            proper = jnp.concatenate([start, value[8:]], axis=0)
        even[x, 0] = proper[:16].astype(BF16)
        even[x, 1:] = narrow[16:].reshape(7, 16, width)
        shifted = jnp.concatenate([tail, proper[: LANES - 8]], axis=0)
        odd[x] = shifted.reshape(8, 16, width).astype(BF16)
        levels = [squares(tail), squares(proper)]
        if last:
            over[x] = jnp.concatenate([bottom, top], axis=0).astype(BF16)
            levels.append(squares(top))
        else:
            edge_out[xx, :8] = bottom
            edge_out[xx, 8:] = top
        level = jnp.concatenate(levels, axis=0)
        new = weight(y, xx) * level
        old = weight(y - 1, xx + 8) * level
        if xx == 0:
            power[slot_now] = new
        else:
            power[slot_now] = power[slot_now] + new
        power[slot_old] = power[slot_old] + old

    raw = [
        rows_of(blocks[0], blocks[1], halos[0][xx], xx, slice(None)).astype(F32)
        for xx in range(8)
    ]
    owned = raw
    rolled = [pltpu.roll(value, 8, 1) for value in owned]
    if not first:
        before = [
            rows_of(before[0], before[1], before_halo_ref[xx], xx, slice(None)).astype(F32)
            for xx in range(8)
        ]
        owned = [jnp.where(lane < 4, before[xx], raw[xx]) for xx in range(8)]
        rolled = [pltpu.roll(value, 8, 1) for value in owned]
        rolled = [
            jnp.where(lane < 8, pltpu.roll(before[xx], 8, 1), rolled[xx]) for xx in range(8)
        ]
    for tile, value in enumerate(block_exchange(owned, lane)):
        left[slot_now, 0, tile] = value
    for tile, value in enumerate(block_exchange(rolled, lane)):
        left[slot_now, 1, tile] = value
    if last:
        total = None
        for xx in range(8):
            value = pltpu.roll(raw[xx], 8 + 16 * xx, 1)
            total = value if total is None else jnp.where(lane // 16 == xx, value, total)
        left_over[slot_now] = total

    @pl.when(y > 0)
    def _():
        o = y - 1
        buffer = lax.rem(o, 2)

        def send(row, which):
            return pltpu.make_async_copy(
                staged.at[which, pl.ds(low, slots - low)],
                sums_ref.at[row, pl.ds(q0, slots - low)],
                sems.at[which],
            )

        @pl.when(o >= 2)
        def _():
            send(o - 2, buffer).wait()

        for i in range(low, slots):
            if i == 16:
                right = over[pl.ds(o * 8, 16)].reshape(256, width)
                sides = [left_over[slot_old], left_over[slot_now]]
            else:
                tile, shift = (i // 2, 1) if i % 2 == 0 else ((i - 1) // 2, 0)
                source = odd if shift else even
                right = source[pl.ds(o * 8, 16), tile].reshape(256, width)
                sides = [left[slot_old, shift, tile], left[slot_now, shift, tile]]
            row = 16 * k + i
            mask = mask_ref[0, row : row + 1, :]
            weighted = (jnp.concatenate(sides, axis=1) * mask).astype(BF16)
            product = jnp.dot(weighted, right, preferred_element_type=F32)
            real = product[:padded, :LANES] + product[padded:, LANES:]
            imag = product[padded:, :LANES] - product[:padded, LANES:]
            energy = jnp.sum(
                cmask_ref[row] * power[slot_old, pl.ds(8 * i, 16), :], axis=0, keepdims=True
            )
            staged[buffer, i, :padded] = real
            staged[buffer, i, padded:] = imag
            staged[buffer, i, padded - 1 : padded] = energy
        send(o, buffer).start()

        @pl.when(o == out_rows - 1)
        def _():
            if out_rows > 1:
                send(o - 1, 1 - buffer).wait()
            send(o, buffer).wait()


def pair_sums(
    k, last, radius, mask, cmask, halos, part, blocks, sources,
    before, before_halo, part_before, edge, sums,
):
    strip_rows, rows2, _ = blocks[0].shape
    rows = strip_rows + 8
    padded = rows2 // 2
    width = 2 * LANES
    out_rows = radius.shape[0]
    first = k == 0
    top = strip_rows // 4 - 1

    def by_rows(array):
        return pl.BlockSpec((8, *array.shape[1:]), lambda y: (y, 0, 0))

    def by_halves(array):
        block = (4, *array.shape[1:])
        return [
            pl.BlockSpec(block, lambda y: (jnp.maximum(2 * y - 1, 0), 0, 0)),
            pl.BlockSpec(block, lambda y: (jnp.minimum(2 * y, top), 0, 0)),
        ]

    def whole(array):
        return pl.BlockSpec(array.shape, lambda y: (0,) * array.ndim)

    def halo_part(number):
        return pl.BlockSpec((8, rows2, LANES), lambda y: (0, number, 0))

    edge_shape = jax.ShapeDtypeStruct((rows, 16, width), F32)
    args = [radius, mask, cmask, *halos]
    in_specs = [
        pl.BlockSpec(memory_space=pltpu.SMEM),
        pl.BlockSpec((1, *mask.shape[1:]), lambda y: (jnp.maximum(y - 1, 0), 0, 0)),
        whole(cmask),
        *[halo_part(part) for _ in halos],
    ]
    for block in blocks:
        args += [block, block]
        in_specs += by_halves(block)
    if not first:
        args += [before, before, before_halo, edge]
        in_specs += [*by_halves(before), halo_part(part_before), by_rows(edge)]
    aliases = {}
    if not first:
        args.append(sums)
        in_specs.append(pl.BlockSpec(memory_space=pl.ANY))
        aliases[len(args) - 1] = 0
    out_cols = cmask.shape[0] - 1
    out_shape = [jax.ShapeDtypeStruct((out_rows, out_cols, rows2, LANES), F32)]
    out_specs = [pl.BlockSpec(memory_space=pl.ANY)]
    if not last:
        out_shape.append(edge_shape)
        out_specs.append(by_rows(edge_shape))
    outs = pl.pallas_call(
        functools.partial(pairs_kernel, k, last, sources, padded),
        grid=(rows // 8,),
        in_specs=in_specs,
        out_specs=out_specs,
        out_shape=out_shape,
        input_output_aliases=aliases,
        scratch_shapes=[
            pltpu.VMEM((rows, 8, 16, width), BF16),
            pltpu.VMEM((rows, 8, 16, width), BF16),
            pltpu.VMEM((rows if last else 8, 16, width), BF16),
            pltpu.VMEM((2, 2, 8, rows2, LANES), F32),
            pltpu.VMEM((2, rows2, LANES), F32),
            pltpu.VMEM((2, 144 if last else 136, LANES), F32),
            pltpu.VMEM((2, 17, rows2, LANES), F32),
            pltpu.SemaphoreType.DMA((2,)),
        ],
        compiler_params=params(),
        name=f"pairs{k}",
        cost_estimate=work(16),
    )(*args)
    return (outs[0], None) if last else (outs[0], outs[1])


def finish_kernel(acqs, padded, groups, me_ref, real_ref, imag_ref, energy_ref, out_ref, power):
    step = pl.program_id(0)
    me = me_ref[0]
    out_rows, out_cols, _, _ = real_ref.shape
    pixels = out_rows * out_cols
    lane_groups = pixels // LANES

    def strided(ref, g, row):
        return ref.reshape(pixels * 8, LANES)[pl.ds(g * LANES * 8 + row, LANES, stride=8), :]

    @pl.when(step == 0)
    def _():
        for g in range(lane_groups):
            power[g] = strided(energy_ref, g, 7).T

    for m in range(8):
        for g in range(lane_groups):
            mine = power[g, pl.ds(step * 8 + m, 1), :]
            scale = lax.rsqrt(power[g] * mine + epsilon)
            for part, ref in enumerate((real_ref, imag_ref)):
                value = strided(ref, g, m).T * scale
                for i in range(groups):
                    start = lax.bitwise_xor(me, i) * (acqs * 2 * lane_groups)
                    out_ref[
                        m, pl.ds(start + 2 * g + part, acqs, stride=2 * lane_groups), :
                    ] = value[i * padded : i * padded + acqs]


def finish(me, sums, acqs, groups):
    out_rows, out_cols, rows2, _ = sums.shape
    padded = rows2 // 2
    lane_groups = out_rows * out_cols // LANES
    total = acqs * groups
    blocks = padded // 8

    def spec(index):
        return pl.BlockSpec((out_rows, out_cols, 8, LANES), index)

    out = pl.pallas_call(
        functools.partial(finish_kernel, acqs, padded, groups),
        grid=(pl.cdiv(acqs, 8),),
        in_specs=[
            pl.BlockSpec(memory_space=pltpu.SMEM),
            spec(lambda i: (0, 0, i, 0)),
            spec(lambda i: (0, 0, i + blocks, 0)),
            spec(lambda i: (0, 0, blocks - 1, 0)),
        ],
        out_specs=pl.BlockSpec((8, total * 2 * lane_groups, LANES), lambda i: (i, 0, 0)),
        out_shape=jax.ShapeDtypeStruct((acqs, total * 2 * lane_groups, LANES), F32),
        scratch_shapes=[pltpu.VMEM((lane_groups, LANES, LANES), F32)],
        compiler_params=params(),
        name="finish",
        cost_estimate=pl.CostEstimate(
            flops=6 * sums.size, bytes_accessed=8 * sums.size, transcendentals=sums.size // 2
        ),
    )(me, sums, sums, sums)
    out = out.reshape(acqs, total, lane_groups, 2, LANES).transpose(0, 1, 3, 2, 4)
    return out.reshape(acqs, total, 2, lane_groups * LANES)


def exchange(value, axis, bit):
    size = lax.axis_size(axis)
    return lax.ppermute(value, axis, [(i, i ^ bit) for i in range(size)])


def neighbours(top, bottom):
    devices = lax.axis_size("strip")
    up = [(i, i + 1) for i in range(devices - 1)]
    down = [(j, i) for i, j in up]
    before = lax.ppermute(bottom, "strip", up)
    after = lax.ppermute(top, "strip", down)
    return jnp.concatenate([before, after], axis=0)


def after(value, *others):
    return lax.optimization_barrier((value, *others))[0]


def gathered(own, padded, filler=()):
    groups = lax.axis_size("acq")
    if groups != 4:
        blocks = [own] + [exchange(own, "acq", bit) for bit in range(1, groups)]
        return blocks, [[(i, part * padded) for i in range(groups)] for part in range(2)]
    one = exchange(own, "acq", 1)
    two = exchange(own, "acq", 2)
    real = exchange(after(two[:, :padded], *filler), "acq", 1)
    imag = exchange(after(one[:, padded:], *filler), "acq", 2)
    blocks = [own, one, two, real, imag]
    shared = [[(i, part * padded) for i in range(3)] for part in range(2)]
    return blocks, [shared[0] + [(3, 0)], shared[1] + [(4, 0)]]


def per_device(
    raw_echo_values,
    cell_target_line,
    cell_track_displacement,
    along_track_chirp_slope,
    along_track_look_radius,
    range_look_radius,
):
    _, strips, cap, acqs, _, columns = raw_echo_values.shape
    groups = lax.axis_size("acq")
    padded = LANES // groups
    out_rows = along_track_look_radius.shape[0]
    out_cols = range_look_radius.shape[0]
    strip_rows = out_rows * 8
    chunks = columns // LANES
    me = lax.axis_index("acq").astype(jnp.int32).reshape(1)

    squared = cell_track_displacement[0].astype(F32) ** 2
    phase = squared[..., None] * along_track_chirp_slope
    cosine, sine = jnp.cos(phase), jnp.sin(phase)
    sent = deramp(raw_echo_values, cosine, sine, [0], cell_target_line[0])
    sent += deramp(raw_echo_values, cosine, sine, list(range(1, chunks)))

    inner = jnp.arange(16, dtype=jnp.int32)
    row_mask = jnp.abs(inner - 8)[None, :] <= along_track_look_radius[:, None]
    column = 8 * jnp.arange(out_cols, dtype=jnp.int32)[:, None] - 4 + inner[None, :]
    col_mask = jnp.abs(inner - 8)[None, :] <= range_look_radius[:, None]
    col_mask = col_mask & (column >= 0) & (column < columns)
    col_mask = jnp.pad(col_mask, ((1, 0), (0, 0)))
    mask = (row_mask[:, None, :, None] & col_mask[None, :, None, :]).astype(F32)
    mask = mask.reshape(out_rows, out_cols + 1, 256)
    cmask = jnp.broadcast_to(col_mask.astype(F32)[:, :, None], (out_cols + 1, 16, LANES))

    received = []

    def receive(k, *others):
        piece = after(sent[k], *others) if others else sent[k]
        received.append(
            lax.all_to_all(piece, "strip", split_axis=0, concat_axis=0, tiled=True)
        )

    def spread(tops, bottoms):
        halo = neighbours(jnp.concatenate(tops, axis=1), jnp.concatenate(bottoms, axis=1))
        return halo, lambda: [halo] + [exchange(halo, "acq", bit) for bit in range(1, groups)]

    common = (along_track_look_radius, mask, cmask)
    owns, tops, bottoms, gathers = [], [], [], []

    def tile(k, *others):
        data = after(received[k], *others) if others else received[k]
        own, top, bottom = make_tile(received[0], data, acqs, padded, strip_rows)
        tops.append(top)
        bottoms.append(bottom)
        return own

    def sums_of(k, halos, part, halos_before, part_before, edge, sums):
        before = owns[k - 1] if k else None
        return pair_sums(
            k, k == chunks - 1, *common, halos, part, *gathers[k],
            before, halos_before, part_before, edge, sums,
        )

    half = chunks // 2
    receive(0)
    for k in range(half):
        receive(k + 1, received[k], *(gathers[k - 1][0] if k else ()))
        owns.append(tile(k))
        gathers.append(gathered(owns[k], padded))
    edges, send_edges = spread(
        [after(top, received[half]) for top in tops],
        [after(bottom, received[half]) for bottom in bottoms],
    )
    edge = sums = None
    early = late = None
    for k in range(half, chunks):
        if k + 1 < chunks:
            receive(k + 1, received[k], edges, *gathers[k - 1][0])
        own = tile(k, edge, *gathers[k - 1][0]) if k > half else tile(k)
        if early is None:
            early = send_edges()
        own = after(own, *early)
        owns.append(own)
        filler = ()
        if k == half:
            for i in range(half):
                sums, edge = sums_of(i, early, i, early[0], i - 1, edge, sums)
                if not filler:
                    filler = (edge,)
        gathers.append(gathered(own, padded, filler))
    edges, send_edges = spread(tops[half:], bottoms[half:])
    late = send_edges()
    for k in range(half, chunks):
        before = (early[0], half - 1) if k == half else (late[0], k - half - 1)
        sums, edge = sums_of(k, late, k - half, *before, edge, sums)
    return finish(me, sums, acqs, groups)


def solution(mesh):
    placed = (
        P("strip", None, None, "acq", None, None),
        P("strip", None, None),
        P("strip", None, None),
        P("acq"),
        P("strip"),
        P(),
    )
    return jax.shard_map(
        per_device,
        mesh=mesh,
        in_specs=placed,
        out_specs=P("acq", None, None, "strip"),
        check_vma=False,
    )
```
